256 devices in a mesh: role: 4 (over z_hi, core), dp: 4 (over x), tensor: 16 (over y, z_lo).
Axes of the slice: x: 4, y: 4, z: 8 (z_hi: 2, z_lo: 4; z = z_hi * 4 + z_lo), core: 2. Of those that a mesh axis runs over, the one named last changes fastest.
Arguments:
- teacher_act: bfloat16 [4, 512, 28672], P(None, 'dp', ('role', 'tensor')), may hold values from -6 to 6
- teacher_down: bfloat16 [28672, 8192], P(('role', 'tensor')), may hold values from -0.09375 to 0.09375
- teacher_resid: bfloat16 [2048, 8192], P(('role', 'dp'), 'tensor'), may hold values from -6 to 6
- attn_out: bfloat16 [2048, 4096], P(('role', 'dp'), 'tensor'), may hold values from -6 to 6
- out_proj: bfloat16 [4096, 4096], P('tensor'), may hold values from -0.09375 to 0.09375
- student_resid: bfloat16 [2048, 4096], P(('role', 'dp')), may hold values from -6 to 6
- proj: bfloat16 [4096, 8192], P(('role', 'dp'), 'tensor'), may hold values from -0.09375 to 0.09375
Outputs:
- attn_grad: bfloat16 [2048, 4096], P(('role', 'dp'), 'tensor')
- proj_grad: float32 [4096, 8192], P(('role', 'dp'), 'tensor')
The draws below stay inside these ranges and needn't reach their ends.
All inputs are finite; a program needn't handle non-finite values.
Results may differ from the reference program's by a relative error of at most 0.024.
Values may be sent and summed in bfloat16 or wider, within the bound.
No kernel may reach another device: no remote copies, remote signals or barrier semaphores. Data moves between devices by JAX's collectives and lax.ppermute only.
A program may use at most 128 MiB of HBM per device.

```python
import math
import jax
import jax.numpy as jnp

D_T = 8192
FF_T = 28672
D_S = 4096
TOK_S = 128
TOKENS = 2048
N_ROLE = 4
N_DP = 4


def strengthened(values, rng, source, target, parts, factor):
    def block_of(axis_at):
        return (jnp.arange(values.shape[axis_at]) // (values.shape[axis_at] // parts)).reshape((-1,) + (1,) * (values.ndim - 1 - axis_at))

    near = jax.random.permutation(rng, parts)[block_of(target)]
    second = (block_of(target) + parts // 2) % parts
    return jnp.where((block_of(source) == near) | (block_of(source) == second), factor * values, values)


def block_levels(stream_key, extent, cuts, low, top_value):
    gain, own = 1.0, jax.random.fold_in(stream_key, 6)
    for dim, parts in cuts:
        draws = jnp.exp(jax.random.uniform(jax.random.fold_in(own, dim), (parts,), jnp.float32, low / len(cuts), top_value / len(cuts)))
        gain = gain * jnp.repeat(draws, extent[dim] // parts).reshape([-1 if axis == dim else 1 for axis in range(len(extent))])
    return gain


def noise(rng, shape, width, limit, pieces=(), held_as=jnp.bfloat16):
    gain = block_levels(rng, shape, pieces, -0.22, 0.18) if pieces else 1.0
    array = jax.random.normal(rng, shape, jnp.float32) * width * gain
    return jnp.minimum(jnp.maximum(array, -limit), limit).astype(held_as)


def bell_draw_with(key, dims, width, limit, cuts, heavy, held_as=jnp.bfloat16):
    values = width * jax.random.normal(key, dims, jnp.float32)
    if cuts:
        values = values * block_levels(key, dims, cuts, -0.22, 0.18)
    return jnp.clip(strengthened(values, jax.random.fold_in(key, 3), *heavy), -limit, limit).astype(held_as)


def setup_inputs(seed: int = 0) -> dict:
    key_list = jax.random.split(jax.random.key(seed), 8)
    return {
        "teacher_act": noise(key_list[0], (N_ROLE, N_DP * TOK_S, FF_T), 1.0, 6.0, ((1, 4), (2, 64))),
        "teacher_down": bell_draw_with(key_list[1], (FF_T, D_T), FF_T ** -0.5, 0.09375, ((0, 64),), (0, 1, 64, 4.0)),
        "teacher_resid": noise(key_list[2], (TOKENS, D_T), 1.0, 6.0, ((0, 16), (1, 16))),
        "attn_out": noise(key_list[3], (TOKENS, D_S), 1.0, 6.0, ((0, 16), (1, 16))),
        "out_proj": noise(key_list[4], (D_S, D_S), D_S ** -0.5, 0.09375, ((0, 16),)),
        "student_resid": bell_draw_with(key_list[5], (TOKENS, D_S), 1.0, 6.0, ((0, 16),), (0, 1, 16, 2.0)),
        "proj": noise(key_list[6], (D_S, D_T), D_S ** -0.5, 0.09375, ((0, 16), (1, 16))),
    }


def reference(teacher_act, teacher_down, teacher_resid, attn_out, out_proj, student_resid, proj):
    flat_act = teacher_act.reshape(TOKENS, FF_T)
    teacher_sum = jnp.dot(flat_act, teacher_down, preferred_element_type=jnp.float32)
    teacher_hidden = (teacher_resid.astype(jnp.float32) + teacher_sum).astype(jnp.bfloat16)
    projected = jnp.dot(attn_out, out_proj, preferred_element_type=jnp.float32)
    student_hidden = (student_resid.astype(jnp.float32) + projected).astype(jnp.bfloat16)
    mapped = jnp.dot(student_hidden, proj, preferred_element_type=jnp.float32)
    err = (mapped - teacher_hidden.astype(jnp.float32)).astype(jnp.bfloat16)
    back = jnp.dot(err, proj.T, preferred_element_type=jnp.float32).astype(jnp.bfloat16)
    attn_grad = jnp.dot(back, out_proj.T, preferred_element_type=jnp.float32).astype(jnp.bfloat16)
    scale_factor = 1.0 / math.sqrt(TOKENS)
    proj_grad = jnp.dot(student_hidden.T, err, preferred_element_type=jnp.float32) * scale_factor
    return (attn_grad, proj_grad)
```

```python
import math

import jax
import jax.numpy as jnp
from jax import lax
from jax.sharding import Mesh
from jax.sharding import PartitionSpec as P

BF = jnp.bfloat16
F32 = jnp.float32
SWAP = [(0, 1), (1, 0)]


def spread(x, axes, dim):
    n = lax.axis_size(axes)
    shape = x.shape
    x = x.reshape(shape[:dim] + (n, shape[dim] // n) + shape[dim + 1 :])
    x = jnp.moveaxis(x, dim, 0)
    return lax.all_to_all(x, axes, 0, 0, tiled=True)


def added(x):
    return jnp.sum(x.astype(F32), axis=0)


def gathered(x, axes):
    n = lax.axis_size(axes)
    return lax.all_to_all(jnp.broadcast_to(x[None], (n,) + x.shape), axes, 0, 0, tiled=True)


def columns(x):
    n, rows, cols = x.shape
    return jnp.moveaxis(x, 0, 1).reshape(rows, n * cols)


def on_device(act, down, t_resid, attn, out_proj, s_resid, proj):
    core = lax.axis_index("c")
    tensor = ("y", "zl")
    tok = attn.shape[0]
    proj_all = lax.all_gather(proj, ("zh", "c", "x"), axis=0, tiled=True)

    act4 = act.reshape(2, 2, tok, act.shape[2])
    theirs = lax.dynamic_index_in_dim(act4, 1 - core, 1, keepdims=False)
    mine = lax.dynamic_index_in_dim(act4, core, 1, keepdims=False)
    sent = jnp.einsum("ksf,fd->ksd", theirs, down, preferred_element_type=F32).astype(BF)
    came = lax.ppermute(sent, "c", SWAP)
    student_part = jnp.dot(attn, out_proj, preferred_element_type=F32).astype(BF)
    own = jnp.einsum("ksf,fd->ksd", mine, down, preferred_element_type=F32)
    chip = (own + came.astype(F32)).astype(BF)
    over_y = added(spread(chip, "y", 2)).astype(BF)
    zh, _, wide = over_y.shape
    zl = lax.axis_size("zl")
    to_z = over_y.reshape(zh, tok, zl, wide // zl)
    to_z = jnp.moveaxis(to_z, 2, 1).reshape(zh * zl, tok, wide // zl)
    teacher_sum = added(lax.all_to_all(to_z, ("zh", "zl"), 0, 0, tiled=True))
    teacher_hidden = (t_resid.astype(F32) + teacher_sum).astype(BF)

    cols = attn.shape[1]
    at = lax.axis_index(tensor) * cols
    resid = lax.dynamic_slice_in_dim(s_resid, at, cols, 1)
    hidden_cols = (resid.astype(F32) + added(spread(student_part, tensor, 1))).astype(BF)
    hidden = columns(gathered(hidden_cols, tensor))

    mapped = jnp.dot(hidden, proj_all, preferred_element_type=F32)
    err = (mapped - teacher_hidden.astype(F32)).astype(BF)

    scale = 1.0 / math.sqrt(tok * 16)
    parts = hidden.reshape(tok, 2, 2, 4 * proj.shape[0])
    h_theirs = lax.dynamic_index_in_dim(parts, 1 - core, 2, keepdims=False).reshape(tok, -1)
    h_mine = lax.dynamic_index_in_dim(parts, core, 2, keepdims=False).reshape(tok, -1)
    contract = (((0,), (0,)), ((), ()))
    g_sent = lax.dot_general(h_theirs, err, contract, preferred_element_type=F32)
    g_came = lax.ppermute((g_sent * scale).astype(BF), "c", SWAP)
    back_part = lax.dot_general(
        err, proj_all, (((1,), (1,)), ((), ())), preferred_element_type=F32
    ).astype(BF)
    g_own = lax.dot_general(h_mine, err, contract, preferred_element_type=F32)
    g_chip = (g_own * scale + g_came.astype(F32)).astype(BF)
    proj_grad = lax.psum_scatter(g_chip, ("zh", "x"), scatter_dimension=0, tiled=True).astype(F32)

    back_cols = added(spread(back_part, tensor, 1)).astype(BF)
    back = columns(gathered(back_cols, tensor))
    attn_grad = lax.dot_general(
        back, out_proj, (((1,), (1,)), ((), ())), preferred_element_type=F32
    ).astype(BF)
    return (attn_grad, proj_grad)


def solution(mesh):
    fine = Mesh(mesh.devices.reshape(2, 2, 4, 4, 4), ("zh", "c", "x", "y", "zl"))
    role, group, tensor = ("zh", "c"), ("zh", "c", "x"), ("y", "zl")
    return jax.shard_map(
        on_device,
        mesh=fine,
        in_specs=(
            P(None, "x", ("zh", "c", "y", "zl")),
            P(("zh", "c", "y", "zl"), None),
            P(group, tensor),
            P(group, tensor),
            P(tensor, None),
            P(group, None),
            P(group, tensor),
        ),
        out_specs=(P(group, tensor), P(group, tensor)),
        check_vma=False,
    )
```

```python
import functools
import math

import jax
import jax.numpy as jnp
from jax import lax
from jax.experimental import pallas as pl
from jax.experimental.pallas import tpu as pltpu
from jax.sharding import Mesh
from jax.sharding import PartitionSpec as P

BF = jnp.bfloat16
F32 = jnp.float32
Z = ("zh", "zl")
NT = (((1,), (1,)), ((), ()))
TN = (((0,), (0,)), ((), ()))
VMEM = pl.BlockSpec(memory_space=pltpu.VMEM)
SMEM = pl.BlockSpec(memory_space=pltpu.SMEM)


COST = pl.CostEstimate(flops=1, bytes_accessed=1, transcendentals=0)


def call(body, outs, args, specs=None):
    return pl.pallas_call(
        body,
        out_shape=outs,
        in_specs=specs or [VMEM] * len(args),
        out_specs=[VMEM] * len(outs),
        compiler_params=pltpu.CompilerParams(vmem_limit_bytes=16 * 2**20),
        cost_estimate=COST,
    )(*args)


def moved_by(x, axes, step):
    n = lax.axis_size(axes)
    return lax.ppermute(x, axes, [(i, (i + step) % n) for i in range(n)])


def swapped(x, axis):
    return lax.ppermute(x, axis, [(0, 1), (1, 0)])


def exchanged(x, axes):
    return lax.all_to_all(x, axes, 0, 0, tiled=True)


def added(x):
    return jnp.sum(x.astype(F32), axis=0)


def teacher_body(at_ref, a_ref, w_ref, their_ref, own_ref, rows_ref):
    tok, width = own_ref.shape[-2:]

    @pl.when(pl.program_id(0) == 0)
    def _():
        for side in range(2):
            for zh in range(2):
                role = zh * 2 + lax.rem(at_ref[1] + 1 - side, 2)
                row = (2 * side + zh) * tok
                rows_ref[row : row + tok, :] = a_ref[role].T

    for zl in range(2):
        block = w_ref[:, zl * width : (zl + 1) * width]
        part = jnp.dot(rows_ref[...], block, preferred_element_type=F32).astype(BF)
        for side, ref in enumerate((their_ref, own_ref)):
            for zh in range(2):
                row = (2 * side + zh) * tok
                ref[0, zh, zl] = part[row : row + tok]


def teacher_terms(at, act, w):
    _, tok, depth = act.shape
    width = w.shape[1] // 16
    shape = jax.ShapeDtypeStruct((4, 2, 4, tok, width), BF)
    out = pl.BlockSpec((1, 2, 2, tok, width), lambda i, at: (i // 2, 0, i % 2, 0, 0))
    terms = pl.pallas_call(
        teacher_body,
        grid_spec=pltpu.PrefetchScalarGridSpec(
            num_scalar_prefetch=1,
            grid=(8,),
            in_specs=[
                pl.BlockSpec((4, depth, tok), lambda i, at: (0, 0, 0)),
                pl.BlockSpec((depth, 2 * width), lambda i, at: (0, lax.rem(at[0] + 2 + i // 2, 4) * 2 + i % 2)),
            ],
            out_specs=[out, out],
            scratch_shapes=[pltpu.VMEM((4 * tok, depth), BF)],
        ),
        out_shape=[shape, shape],
        compiler_params=pltpu.CompilerParams(vmem_limit_bytes=56 * 2**20),
        cost_estimate=COST,
    )(at, jnp.swapaxes(act, 1, 2), w)
    return [t.reshape(4, 8, tok, width) for t in terms]


def student_body(a_ref, w_ref, o_ref):
    width = o_ref.shape[-1]
    for i in range(16):
        block = w_ref[:, i * width : (i + 1) * width]
        o_ref[i // 4, i % 4] = jnp.dot(a_ref[...], block, preferred_element_type=F32).astype(BF)


def hidden_body(x_ref, resid_ref, o_ref):
    hidden = (resid_ref[...].astype(F32) + added(x_ref[...])).astype(BF)
    for i in range(o_ref.shape[0]):
        o_ref[i] = hidden


def mapped_body(at_ref, h_ref, one_ref, two_ref, out_ref):
    total = None
    for i in range(16):
        block = (one_ref, two_ref)[i // 8][i % 8]
        term = jnp.dot(h_ref[at_ref[i]], block, preferred_element_type=F32)
        total = term if total is None else total + term
    out_ref[...] = total


def err_body(at_ref, mapped_ref, resid_ref, terms_ref, one_ref, two_ref, err_ref, back_ref):
    teacher = (resid_ref[...].astype(F32) + added(terms_ref[...])).astype(BF)
    err = (mapped_ref[...] - teacher.astype(F32)).astype(BF)
    err_ref[...] = err
    for i in range(16):
        block = (one_ref, two_ref)[i // 8][i % 8]
        at = at_ref[i]
        back = lax.dot_general(err, block, NT, preferred_element_type=F32)
        back_ref[at // 4, lax.rem(at, 4)] = back.astype(BF)


def grad_body(scale, first, at_ref, h_ref, err_ref, *refs):
    err = err_ref[...]
    outs = refs[-4:] if first == 0 else refs
    for i in range(8):
        term = lax.dot_general(h_ref[at_ref[first + i]], err, TN, preferred_element_type=F32) * scale
        if first == 0:
            outs[i // 2][i % 2] = (term + refs[0][i].astype(F32)).astype(BF)
        else:
            outs[0][i] = term.astype(BF)


def grad_sum_body(*refs):
    terms, (own_ref, sent_ref) = refs[:-2], refs[-2:]
    for z, ref in enumerate((own_ref, sent_ref)):
        total = terms[0][z].astype(F32)
        for term in terms[1:]:
            total = total + term[z].astype(F32)
        ref[...] = total.astype(ref.dtype)


def sum_body(x_ref, o_ref):
    total = x_ref[0].astype(F32)
    for i in range(1, x_ref.shape[0]):
        total = total + x_ref[i].astype(F32)
    total = total.astype(BF)
    for i in range(o_ref.shape[0]):
        o_ref[i] = total


def terms_body(*refs):
    total = refs[0][...].astype(F32)
    for ref in refs[1:-1]:
        total = total + ref[...].astype(F32)
    refs[-1][...] = total.astype(BF)


def attn_body(y_ref, w_ref, *refs):
    back_refs, o_ref = refs[:-1], refs[-1]
    total = None
    cols = back_refs[0].shape[-1]
    for step in range(4):
        for zl in range(4):
            at = pl.multiple_of((lax.rem(y_ref[0] + step, 4) * 4 + zl) * cols, cols)
            block = w_ref[:, pl.ds(at, cols)]
            term = lax.dot_general(back_refs[step][zl], block, NT, preferred_element_type=F32)
            total = term if total is None else total + term
    o_ref[...] = total.astype(BF)


def tied(*arrays):
    return lax.optimization_barrier(arrays)


def on_device(act, down, t_resid, attn, out_proj, s_resid, proj):
    core, zh, x, y = (lax.axis_index(a) for a in ("c", "zh", "x", "y"))
    tok, cols = attn.shape
    tensor = ("y", "zl")
    plus = lambda a, b: a.astype(F32) + b.astype(F32)
    shape = lambda *dims, dtype=BF: jax.ShapeDtypeStruct(dims, dtype)
    here = jnp.stack([y, core]).astype(jnp.int32)

    proj_z = swapped(proj, "zh")
    rows_x = [proj] + [moved_by(proj, "x", -step) for step in (1, 2, 3)]
    idx = jnp.stack(
        [
            ((zh + dz) % 2 * 2 + (core + dc) % 2) * 4 + (x + dx) % 4
            for dc in range(2)
            for dx in range(4)
            for dz in range(2)
        ]
    ).astype(jnp.int32)
    at_cols = (idx // 4 - y + 4) % 4 * 4 + idx % 4

    at = lax.axis_index(tensor) * cols
    resid = lax.dynamic_slice_in_dim(s_resid, at, cols, 1)
    part = call(student_body, [shape(4, 4, tok, cols)], [attn, out_proj])[0]
    act, part = tied(act, part)
    student = exchanged(part, "y")

    sent, mine = teacher_terms(here, act, down)
    student = call(sum_body, [shape(1, 4, tok, cols)], [student])[0][0]
    sent, student = tied(sent, student)
    came = swapped(sent, "c")
    up, down_ = plus(mine[0, :4], came[0, :4]).astype(BF), plus(mine[0, 4:], came[0, 4:]).astype(BF)
    up, down_, proj_z = tied(up, down_, proj_z)
    up, down_ = tied(moved_by(up, "y", 1), moved_by(down_, "y", -1))
    rows_z = [proj_z] + [moved_by(proj_z, "x", -step) for step in (1, 2, 3)]
    student = exchanged(student, "zl")
    near = plus(mine[3], came[3])
    up = jnp.concatenate([near[:4] + up.astype(F32), near[4:]], axis=0).astype(BF)
    near = plus(mine[1], came[1])
    down_ = jnp.concatenate([near[:4], near[4:] + down_.astype(F32)], axis=0).astype(BF)
    hidden = call(hidden_body, [shape(4, tok, cols)], [student, resid])[0]
    hidden = exchanged(hidden, "zl")
    up, down_, hidden, *rows_x, rows_z[0], rows_z[1], rows_z[2], rows_z[3] = tied(
        up, down_, hidden, *rows_x, *rows_z
    )
    up, down_ = tied(moved_by(up, "y", 1), moved_by(down_, "y", -1))
    over_y = (plus(mine[2], came[2]) + plus(up, down_)).astype(BF)
    terms = exchanged(over_y, Z)
    rows = jnp.stack([r for both in zip(rows_x, rows_z) for r in both])
    rows = [rows, swapped(rows, "c")]
    hidden = jnp.concatenate([hidden] + [moved_by(hidden, "y", -step) for step in (1, 2, 3)], axis=0)

    mapped = call(
        mapped_body,
        [shape(*t_resid.shape, dtype=F32)],
        [at_cols, hidden, *rows],
        [SMEM, VMEM, VMEM, VMEM],
    )[0]
    mapped, terms = tied(mapped, terms)
    err, back = call(
        err_body,
        [shape(*t_resid.shape), shape(4, 4, tok, cols)],
        [at_cols, mapped, t_resid, terms, *rows],
        [SMEM] + [VMEM] * 5,
    )
    back_moved = [moved_by(back[step], "y", step) for step in (1, 2, 3)]

    scale = 1.0 / math.sqrt(tok * 16)
    theirs_g = call(
        functools.partial(grad_body, scale, 8),
        [shape(8, *proj.shape)],
        [at_cols, hidden, err],
        [SMEM, VMEM, VMEM],
    )[0]
    came_g = swapped(theirs_g, "c")
    chip_g = call(
        functools.partial(grad_body, scale, 0),
        [shape(2, *proj.shape)] * 4,
        [at_cols, hidden, err, came_g],
        [SMEM, VMEM, VMEM, VMEM],
    )
    moved_g = [moved_by(chip_g[step], "x", step) for step in (1, 2, 3)]

    back_moved[0], _ = tied(back_moved[0], chip_g[0])
    back = call(terms_body, [shape(4, tok, cols)], [back[0], *back_moved])[0]
    back = exchanged(back, "zl")
    back = call(sum_body, [shape(4, tok, cols)], [back])[0]
    back = exchanged(back, "zl")
    back, *moved_g = tied(back, *moved_g)
    back_all = [back] + [moved_by(back, "y", -step) for step in (1, 2, 3)]

    own_g, sent_g = call(
        grad_sum_body, [shape(*proj.shape, dtype=F32), shape(*proj.shape)], [chip_g[0], *moved_g]
    )
    came_g = swapped(sent_g, "zh")
    attn_grad = call(attn_body, [shape(tok, cols)], [here, out_proj, *back_all], [SMEM] + [VMEM] * 5)[0]
    attn_grad, came_g = tied(attn_grad, came_g)
    proj_grad = own_g + came_g.astype(F32)
    return (attn_grad, proj_grad)


def solution(mesh):
    fine = Mesh(mesh.devices.reshape(2, 2, 4, 4, 4), ("zh", "c", "x", "y", "zl"))
    group, tensor = ("zh", "c", "x"), ("y", "zl")
    hidden_units = ("zh", "c", "y", "zl")
    return jax.shard_map(
        on_device,
        mesh=fine,
        in_specs=(
            P(None, "x", hidden_units),
            P(hidden_units, None),
            P(group, tensor),
            P(group, tensor),
            P(tensor, None),
            P(group, None),
            P(group, tensor),
        ),
        out_specs=(P(group, tensor), P(group, tensor)),
        check_vma=False,
    )
```

```python
import functools
import math

import jax
import jax.numpy as jnp
from jax import lax
from jax.experimental import pallas as pl
from jax.experimental.pallas import tpu as pltpu
from jax.sharding import Mesh
from jax.sharding import PartitionSpec as P

BF = jnp.bfloat16
F32 = jnp.float32
Z = ("zh", "zl")
NT = (((1,), (1,)), ((), ()))
TN = (((0,), (0,)), ((), ()))
VMEM = pl.BlockSpec(memory_space=pltpu.VMEM)
SMEM = pl.BlockSpec(memory_space=pltpu.SMEM)


COST = pl.CostEstimate(flops=1, bytes_accessed=1, transcendentals=0)


def call(body, outs, args, specs=None):
    return pl.pallas_call(
        body,
        out_shape=outs,
        in_specs=specs or [VMEM] * len(args),
        out_specs=[VMEM] * len(outs),
        compiler_params=pltpu.CompilerParams(vmem_limit_bytes=16 * 2**20),
        cost_estimate=COST,
    )(*args)


def moved_by(x, axes, step):
    n = lax.axis_size(axes)
    return lax.ppermute(x, axes, [(i, (i + step) % n) for i in range(n)])


def swapped(x, axis):
    return lax.ppermute(x, axis, [(0, 1), (1, 0)])


def exchanged(x, axes):
    return lax.all_to_all(x, axes, 0, 0, tiled=True)


def added(x):
    return jnp.sum(x.astype(F32), axis=0)


def teacher_body(at_ref, a_ref, w_ref, their_ref, own_ref, rows_ref):
    tok, width = own_ref.shape[-2:]

    @pl.when(pl.program_id(0) == 0)
    def _():
        for side in range(2):
            for zh in range(2):
                role = zh * 2 + lax.rem(at_ref[1] + 1 - side, 2)
                row = (2 * side + zh) * tok
                rows_ref[row : row + tok, :] = a_ref[role].T

    for zl in range(2):
        block = w_ref[:, zl * width : (zl + 1) * width]
        part = jnp.dot(rows_ref[...], block, preferred_element_type=F32).astype(BF)
        for side, ref in enumerate((their_ref, own_ref)):
            for zh in range(2):
                row = (2 * side + zh) * tok
                ref[0, zh, zl] = part[row : row + tok]


def teacher_terms(at, act, w, first, count):
    _, tok, depth = act.shape
    width = w.shape[1] // 16
    shape = jax.ShapeDtypeStruct((count, 2, 4, tok, width), BF)
    out = pl.BlockSpec((1, 2, 2, tok, width), lambda i, at: (i // 2, 0, i % 2, 0, 0))
    terms = pl.pallas_call(
        teacher_body,
        grid_spec=pltpu.PrefetchScalarGridSpec(
            num_scalar_prefetch=1,
            grid=(2 * count,),
            in_specs=[
                pl.BlockSpec((4, depth, tok), lambda i, at: (0, 0, 0)),
                pl.BlockSpec((depth, 2 * width), lambda i, at: (0, lax.rem(at[0] + first + i // 2, 4) * 2 + i % 2)),
            ],
            out_specs=[out, out],
            scratch_shapes=[pltpu.VMEM((4 * tok, depth), BF)],
        ),
        out_shape=[shape, shape],
        compiler_params=pltpu.CompilerParams(vmem_limit_bytes=56 * 2**20),
        cost_estimate=COST,
    )(at, jnp.swapaxes(act, 1, 2), w)
    return [t.reshape(count, 8, tok, width) for t in terms]


def far_body(mine_ref, came_ref, up_ref, down_ref):
    half = up_ref.shape[0]
    total = mine_ref[0].astype(F32) + came_ref[0].astype(F32)
    up_ref[...] = total[:half].astype(BF)
    down_ref[...] = total[half:].astype(BF)


def chip_body(*refs):
    for k in range(3):
        refs[6 + k][...] = (refs[2 * k][0].astype(F32) + refs[2 * k + 1][0].astype(F32)).astype(BF)


def near_body(near_up, near_down, far_up, far_down, up_ref, down_ref):
    half = far_up.shape[0]
    up_ref[:half] = (near_up[:half].astype(F32) + far_up[...].astype(F32)).astype(BF)
    up_ref[half:] = near_up[half:]
    down_ref[:half] = near_down[:half]
    down_ref[half:] = (near_down[half:].astype(F32) + far_down[...].astype(F32)).astype(BF)


def on_blocks(body, outs, blocks):
    def spec(shape, at):
        return pl.BlockSpec(shape, lambda i: at)

    return pl.pallas_call(
        body,
        grid=(1,),
        in_specs=[spec(shape, at) for _, shape, at in blocks],
        out_specs=[spec(o.shape, (0,) * len(o.shape)) for o in outs],
        out_shape=outs,
        compiler_params=pltpu.CompilerParams(vmem_limit_bytes=56 * 2**20),
        cost_estimate=COST,
    )(*[a for a, _, _ in blocks])


def student_body(a_ref, w_ref, o_ref):
    width = o_ref.shape[-1]
    for i in range(16):
        block = w_ref[:, i * width : (i + 1) * width]
        o_ref[i // 4, i % 4] = jnp.dot(a_ref[...], block, preferred_element_type=F32).astype(BF)


def hidden_body(x_ref, resid_ref, o_ref):
    hidden = (resid_ref[...].astype(F32) + added(x_ref[...])).astype(BF)
    for i in range(o_ref.shape[0]):
        o_ref[i] = hidden


def block_of(refs, i):
    pair, next_, last_, far_one, far_two = refs[5 * (i // 8) : 5 * (i // 8) + 5]
    x, z = i % 8 // 2, i % 2
    if x == 2:
        return (far_one, far_two)[z][...]
    return {0: pair, 1: next_, 3: last_}[x][z]


def mapped_body(at_ref, h_ref, *refs):
    out_ref, rows_ref = refs[-2:]
    total = None
    for i in range(16):
        block = block_of(refs, i)
        rows_ref[i] = block
        term = jnp.dot(h_ref[at_ref[i]], block, preferred_element_type=F32)
        total = term if total is None else total + term
    out_ref[...] = total


def err_body(at_ref, mapped_ref, resid_ref, terms_ref, rows_ref, err_ref, back_ref):
    teacher = (resid_ref[...].astype(F32) + added(terms_ref[...])).astype(BF)
    err_ref[...] = (mapped_ref[...] - teacher.astype(F32)).astype(BF)
    err = err_ref[...]
    for i in range(16):
        at = at_ref[i]
        back = lax.dot_general(err, rows_ref[i], NT, preferred_element_type=F32)
        back_ref[at // 4, lax.rem(at, 4)] = back.astype(BF)


def grad_body(scale, first, at_ref, h_ref, err_ref, *refs):
    err = err_ref[...]
    if first == 0:
        near, left, right, far_up, far_down = refs[1:]
        outs = [near.at[0], near.at[1], left.at[0], left.at[1], far_up, far_down, right.at[0], right.at[1]]
    for i in range(8):
        term = lax.dot_general(h_ref[at_ref[first + i]], err, TN, preferred_element_type=F32) * scale
        if first == 0:
            outs[i][...] = (term + refs[0][i].astype(F32)).astype(BF)
        else:
            refs[0][i] = term.astype(BF)


def grad_near_body(left_ref, right_ref, up_ref, down_ref, up_out, down_out):
    up_out[0] = (left_ref[0].astype(F32) + up_ref[...].astype(F32)).astype(BF)
    up_out[1] = left_ref[1]
    down_out[0] = right_ref[0]
    down_out[1] = (right_ref[1].astype(F32) + down_ref[...].astype(F32)).astype(BF)


def grad_sum_body(*refs):
    terms, (own_ref, sent_ref) = refs[:-2], refs[-2:]
    for z, ref in enumerate((own_ref, sent_ref)):
        total = terms[0][z].astype(F32)
        for term in terms[1:]:
            total = total + term[z].astype(F32)
        ref[...] = total.astype(ref.dtype)


def sum_body(x_ref, o_ref):
    total = x_ref[0].astype(F32)
    for i in range(1, x_ref.shape[0]):
        total = total + x_ref[i].astype(F32)
    total = total.astype(BF)
    for i in range(o_ref.shape[0]):
        o_ref[i] = total


def terms_body(*refs):
    total = refs[0][...].astype(F32)
    for ref in refs[1:-1]:
        total = total + ref[...].astype(F32)
    refs[-1][...] = total.astype(BF)


def attn_body(y_ref, w_ref, *refs):
    back_refs, o_ref = refs[:-1], refs[-1]
    total = None
    cols = back_refs[0].shape[-1]
    for step in range(4):
        for zl in range(4):
            at = pl.multiple_of((lax.rem(y_ref[0] + step, 4) * 4 + zl) * cols, cols)
            block = w_ref[:, pl.ds(at, cols)]
            term = lax.dot_general(back_refs[step][zl], block, NT, preferred_element_type=F32)
            total = term if total is None else total + term
    o_ref[...] = total.astype(BF)


def tied(*arrays):
    return lax.optimization_barrier(arrays)


def on_device(act, down, t_resid, attn, out_proj, s_resid, proj):
    core, zh, x, y = (lax.axis_index(a) for a in ("c", "zh", "x", "y"))
    tok, cols = attn.shape
    tensor = ("y", "zl")
    plus = lambda a, b: a.astype(F32) + b.astype(F32)
    shape = lambda *dims, dtype=BF: jax.ShapeDtypeStruct(dims, dtype)
    here = jnp.stack([y, core]).astype(jnp.int32)

    pair = jnp.stack([proj, swapped(proj, "zh")])
    idx = jnp.stack(
        [
            ((zh + dz) % 2 * 2 + (core + dc) % 2) * 4 + (x + dx) % 4
            for dc in range(2)
            for dx in range(4)
            for dz in range(2)
        ]
    ).astype(jnp.int32)
    at_cols = (idx // 4 - y + 4) % 4 * 4 + idx % 4

    at = lax.axis_index(tensor) * cols
    resid = lax.dynamic_slice_in_dim(s_resid, at, cols, 1)
    part = call(student_body, [shape(4, 4, tok, cols)], [attn, out_proj])[0]
    act, part = tied(act, part)
    student = exchanged(part, "y")

    sent, mine = teacher_terms(here, act, down, 2, 4)
    student = call(sum_body, [shape(1, 4, tok, cols)], [student])[0][0]
    sent, student = tied(sent, student)
    came = swapped(sent, "c")
    student = exchanged(student, "zl")
    width = t_resid.shape[1]
    piece = (1, 8, tok, width)
    blocks = [(a, piece, (0, 0, 0, 0)) for a in (mine, came)]
    up, down_ = on_blocks(far_body, [shape(4, tok, width)] * 2, blocks)
    up, down_ = tied(moved_by(up, "y", 1), moved_by(down_, "y", -1))
    blocks = [(a, piece, (d, 0, 0, 0)) for d in (3, 1, 2) for a in (mine, came)]
    near_up, near_down, chip = on_blocks(chip_body, [shape(8, tok, width)] * 3, blocks)
    student, near_up, near_down, chip = tied(student, near_up, near_down, chip)
    hidden = call(hidden_body, [shape(4, tok, cols)], [student, resid])[0]
    ups = call(near_body, [shape(8, tok, width)] * 2, [near_up, near_down, up, down_])
    hidden, *ups = tied(hidden, *ups)
    hidden = exchanged(hidden, "zl")
    pair = tied(pair, hidden)[0]
    ups = tied(moved_by(ups[0], "y", 1), moved_by(ups[1], "y", -1))

    next_, last_ = tied(moved_by(pair, "x", -1), moved_by(pair, "x", 1))
    far_rows = tied(moved_by(next_[0], "x", -1), moved_by(last_[1], "x", 1))

    over = call(terms_body, [shape(8, tok, width)], [chip, *ups])[0]
    over, hidden = tied(over, hidden)
    terms = exchanged(over, Z)
    hidden = jnp.concatenate(
        [hidden, *tied(*(moved_by(hidden, "y", -step) for step in (1, 2, 3)))], axis=0
    )
    rows = [pair, next_, last_, *far_rows]
    rows = rows + [swapped(r, "c") for r in rows]

    mapped, rows = call(
        mapped_body,
        [shape(*t_resid.shape, dtype=F32), shape(16, *proj.shape)],
        [at_cols, hidden, *rows],
        [SMEM] + [VMEM] * 11,
    )
    mapped, terms = tied(mapped, terms)
    err, back = call(
        err_body,
        [shape(*t_resid.shape), shape(4, 4, tok, cols)],
        [at_cols, mapped, t_resid, terms, rows],
        [SMEM] + [VMEM] * 4,
    )
    back_moved = tied(*(moved_by(back[step], "y", step) for step in (1, 2, 3)))

    scale = 1.0 / math.sqrt(tok * 16)
    theirs_g = call(
        functools.partial(grad_body, scale, 8),
        [shape(8, *proj.shape)],
        [at_cols, hidden, err],
        [SMEM, VMEM, VMEM],
    )[0]
    came_g = swapped(theirs_g, "c")
    near_g, left_g, right_g, far_up, far_down = call(
        functools.partial(grad_body, scale, 0),
        [shape(2, *proj.shape)] * 3 + [shape(*proj.shape)] * 2,
        [at_cols, hidden, err, came_g],
        [SMEM, VMEM, VMEM, VMEM],
    )
    far_up, far_down = moved_by(far_up, "x", 1), moved_by(far_down, "x", -1)
    moved_g = call(grad_near_body, [shape(2, *proj.shape)] * 2, [left_g, right_g, far_up, far_down])
    *back_moved, up_g, down_g = tied(*back_moved, *moved_g)
    moved_g = [up_g, down_g]
    moved_g = [moved_by(moved_g[0], "x", 1), moved_by(moved_g[1], "x", -1)]

    back = call(terms_body, [shape(4, tok, cols)], [back[0], *back_moved])[0]
    back = exchanged(back, "zl")
    back = call(sum_body, [shape(4, tok, cols)], [back])[0]
    back = exchanged(back, "zl")
    back, *moved_g = tied(back, *moved_g)
    back_all = [back, *tied(*(moved_by(back, "y", -step) for step in (1, 2, 3)))]

    own_g, sent_g = call(
        grad_sum_body, [shape(*proj.shape, dtype=F32), shape(*proj.shape)], [near_g, *moved_g]
    )
    came_g = swapped(sent_g, "zh")
    attn_grad = call(attn_body, [shape(tok, cols)], [here, out_proj, *back_all], [SMEM] + [VMEM] * 5)[0]
    attn_grad, came_g = tied(attn_grad, came_g)
    proj_grad = own_g + came_g.astype(F32)
    return (attn_grad, proj_grad)


def solution(mesh):
    fine = Mesh(mesh.devices.reshape(2, 2, 4, 4, 4), ("zh", "c", "x", "y", "zl"))
    group, tensor = ("zh", "c", "x"), ("y", "zl")
    hidden_units = ("zh", "c", "y", "zl")
    return jax.shard_map(
        on_device,
        mesh=fine,
        in_specs=(
            P(None, "x", hidden_units),
            P(hidden_units, None),
            P(group, tensor),
            P(group, tensor),
            P(tensor, None),
            P(group, None),
            P(group, tensor),
        ),
        out_specs=(P(group, tensor), P(group, tensor)),
        check_vma=False,
    )
```

```python
import functools
import math

import jax
import jax.numpy as jnp
from jax import lax
from jax.experimental import pallas as pl
from jax.experimental.pallas import tpu as pltpu
from jax.sharding import Mesh
from jax.sharding import PartitionSpec as P

BF = jnp.bfloat16
F32 = jnp.float32
Z = ("zh", "zl")
NT = (((1,), (1,)), ((), ()))
TN = (((0,), (0,)), ((), ()))
VMEM = pl.BlockSpec(memory_space=pltpu.VMEM)
SMEM = pl.BlockSpec(memory_space=pltpu.SMEM)


COST = pl.CostEstimate(flops=1, bytes_accessed=1, transcendentals=0)


def call(body, outs, args, specs=None):
    return pl.pallas_call(
        body,
        out_shape=outs,
        in_specs=specs or [VMEM] * len(args),
        out_specs=[VMEM] * len(outs),
        compiler_params=pltpu.CompilerParams(vmem_limit_bytes=16 * 2**20),
        cost_estimate=COST,
    )(*args)


def moved_by(x, axes, step):
    n = lax.axis_size(axes)
    return lax.ppermute(x, axes, [(i, (i + step) % n) for i in range(n)])


def swapped(x, axis):
    return lax.ppermute(x, axis, [(0, 1), (1, 0)])


def exchanged(x, axes):
    return lax.all_to_all(x, axes, 0, 0, tiled=True)


def added(x):
    return jnp.sum(x.astype(F32), axis=0)


def teacher_body(at_ref, a_ref, w_ref, their_ref, own_ref, rows_ref):
    tok, width = own_ref.shape[-2:]

    @pl.when(pl.program_id(0) == 0)
    def _():
        for side in range(2):
            for zh in range(2):
                role = zh * 2 + lax.rem(at_ref[1] + 1 - side, 2)
                row = (2 * side + zh) * tok
                rows_ref[row : row + tok, :] = a_ref[role].T

    for zl in range(2):
        block = w_ref[:, zl * width : (zl + 1) * width]
        part = jnp.dot(rows_ref[...], block, preferred_element_type=F32).astype(BF)
        for side, ref in enumerate((their_ref, own_ref)):
            for zh in range(2):
                row = (2 * side + zh) * tok
                ref[0, zh, zl] = part[row : row + tok]


def teacher_terms(at, act, w, first, count):
    _, tok, depth = act.shape
    width = w.shape[1] // 16
    shape = jax.ShapeDtypeStruct((count, 2, 4, tok, width), BF)
    out = pl.BlockSpec((1, 2, 2, tok, width), lambda i, at: (i // 2, 0, i % 2, 0, 0))
    terms = pl.pallas_call(
        teacher_body,
        grid_spec=pltpu.PrefetchScalarGridSpec(
            num_scalar_prefetch=1,
            grid=(2 * count,),
            in_specs=[
                pl.BlockSpec((4, depth, tok), lambda i, at: (0, 0, 0)),
                pl.BlockSpec((depth, 2 * width), lambda i, at: (0, lax.rem(at[0] + first + i // 2, 4) * 2 + i % 2)),
            ],
            out_specs=[out, out],
            scratch_shapes=[pltpu.VMEM((4 * tok, depth), BF)],
        ),
        out_shape=[shape, shape],
        compiler_params=pltpu.CompilerParams(vmem_limit_bytes=56 * 2**20),
        cost_estimate=COST,
    )(at, jnp.swapaxes(act, 1, 2), w)
    return [t.reshape(count, 8, tok, width) for t in terms]


def far_body(mine_ref, came_ref, up_ref, down_ref):
    half = up_ref.shape[0]
    total = mine_ref[0].astype(F32) + came_ref[0].astype(F32)
    up_ref[...] = total[:half].astype(BF)
    down_ref[...] = total[half:].astype(BF)


def chip_body(*refs):
    for k in range(3):
        refs[6 + k][...] = (refs[2 * k][0].astype(F32) + refs[2 * k + 1][0].astype(F32)).astype(BF)


def near_body(near_up, near_down, far_up, far_down, up_ref, down_ref):
    half = far_up.shape[0]
    up_ref[:half] = (near_up[:half].astype(F32) + far_up[...].astype(F32)).astype(BF)
    up_ref[half:] = near_up[half:]
    down_ref[:half] = near_down[:half]
    down_ref[half:] = (near_down[half:].astype(F32) + far_down[...].astype(F32)).astype(BF)


def on_blocks(body, outs, blocks):
    def spec(shape, at):
        return pl.BlockSpec(shape, lambda i: at)

    return pl.pallas_call(
        body,
        grid=(1,),
        in_specs=[spec(shape, at) for _, shape, at in blocks],
        out_specs=[spec(o.shape, (0,) * len(o.shape)) for o in outs],
        out_shape=outs,
        compiler_params=pltpu.CompilerParams(vmem_limit_bytes=56 * 2**20),
        cost_estimate=COST,
    )(*[a for a, _, _ in blocks])


def student_body(a_ref, w_ref, o_ref):
    width = o_ref.shape[-1]
    for i in range(16):
        block = w_ref[:, i * width : (i + 1) * width]
        o_ref[i // 4, i % 4] = jnp.dot(a_ref[...], block, preferred_element_type=F32).astype(BF)


def hidden_body(x_ref, resid_ref, o_ref):
    hidden = (resid_ref[...].astype(F32) + added(x_ref[...])).astype(BF)
    for i in range(o_ref.shape[0]):
        o_ref[i] = hidden


def block_of(refs, i):
    pair, next_, last_, far_one, far_two = refs[5 * (i // 8) : 5 * (i // 8) + 5]
    x, z = i % 8 // 2, i % 2
    if x == 2:
        return (far_one, far_two)[z][...]
    return {0: pair, 1: next_, 3: last_}[x][z]


def mapped_body(at_ref, h_ref, *refs):
    out_ref, rows_ref = refs[-2:]
    total = None
    for i in range(16):
        block = block_of(refs, i)
        rows_ref[i] = block
        term = jnp.dot(h_ref[at_ref[i]], block, preferred_element_type=F32)
        total = term if total is None else total + term
    out_ref[...] = total


def err_body(at_ref, mapped_ref, resid_ref, terms_ref, rows_ref, err_ref, back_ref):
    teacher = (resid_ref[...].astype(F32) + added(terms_ref[...])).astype(BF)
    err_ref[...] = (mapped_ref[...] - teacher.astype(F32)).astype(BF)
    err = err_ref[...]
    for i in range(16):
        at = at_ref[i]
        back = lax.dot_general(err, rows_ref[i], NT, preferred_element_type=F32)
        back_ref[at // 4, lax.rem(at, 4)] = back.astype(BF)


def grad_body(scale, first, at_ref, h_ref, err_ref, *refs):
    err = err_ref[...]
    if first == 0:
        near, left, right, far_up, far_down = refs[1:]
        outs = [near.at[0], near.at[1], left.at[0], left.at[1], far_up, far_down, right.at[0], right.at[1]]
    for i in range(8):
        term = lax.dot_general(h_ref[at_ref[first + i]], err, TN, preferred_element_type=F32) * scale
        if first == 0:
            outs[i][...] = (term + refs[0][i].astype(F32)).astype(BF)
        else:
            refs[0][i] = term.astype(BF)


def grad_near_body(left_ref, right_ref, up_ref, down_ref, up_out, down_out):
    up_out[0] = (left_ref[0].astype(F32) + up_ref[...].astype(F32)).astype(BF)
    up_out[1] = left_ref[1]
    down_out[0] = right_ref[0]
    down_out[1] = (right_ref[1].astype(F32) + down_ref[...].astype(F32)).astype(BF)


def grad_sum_body(*refs):
    terms, (own_ref, sent_ref) = refs[:-2], refs[-2:]
    for z, ref in enumerate((own_ref, sent_ref)):
        total = terms[0][z].astype(F32)
        for term in terms[1:]:
            total = total + term[z].astype(F32)
        ref[...] = total.astype(ref.dtype)


def sum_body(x_ref, o_ref):
    total = x_ref[0].astype(F32)
    for i in range(1, x_ref.shape[0]):
        total = total + x_ref[i].astype(F32)
    total = total.astype(BF)
    for i in range(o_ref.shape[0]):
        o_ref[i] = total


def terms_body(*refs):
    total = refs[0][...].astype(F32)
    for ref in refs[1:-1]:
        total = total + ref[...].astype(F32)
    refs[-1][...] = total.astype(BF)


def attn_body(y_ref, w_ref, *refs):
    back_refs, o_ref = refs[:-1], refs[-1]
    total = None
    cols = back_refs[0].shape[-1]
    for step in range(4):
        for zl in range(4):
            at = pl.multiple_of((lax.rem(y_ref[0] + step, 4) * 4 + zl) * cols, cols)
            block = w_ref[:, pl.ds(at, cols)]
            term = lax.dot_general(back_refs[step][zl], block, NT, preferred_element_type=F32)
            total = term if total is None else total + term
    o_ref[...] = total.astype(BF)


def tied(*arrays):
    return lax.optimization_barrier(arrays)


def on_device(act, down, t_resid, attn, out_proj, s_resid, proj):
    core, zh, x, y = (lax.axis_index(a) for a in ("c", "zh", "x", "y"))
    tok, cols = attn.shape
    tensor = ("y", "zl")
    plus = lambda a, b: a.astype(F32) + b.astype(F32)
    shape = lambda *dims, dtype=BF: jax.ShapeDtypeStruct(dims, dtype)
    here = jnp.stack([y, core]).astype(jnp.int32)

    pair = jnp.stack([proj, swapped(proj, "zh")])
    idx = jnp.stack(
        [
            ((zh + dz) % 2 * 2 + (core + dc) % 2) * 4 + (x + dx) % 4
            for dc in range(2)
            for dx in range(4)
            for dz in range(2)
        ]
    ).astype(jnp.int32)
    at_cols = (idx // 4 - y + 4) % 4 * 4 + idx % 4

    at = lax.axis_index(tensor) * cols
    resid = lax.dynamic_slice_in_dim(s_resid, at, cols, 1)
    part = call(student_body, [shape(4, 4, tok, cols)], [attn, out_proj])[0]
    act, part = tied(act, part)
    student = exchanged(part, "y")

    sent, mine = teacher_terms(here, act, down, 2, 4)
    student = call(sum_body, [shape(1, 4, tok, cols)], [student])[0][0]
    sent, student, pair = tied(sent, student, pair)
    came = swapped(sent, "c")
    student = exchanged(student, "zl")
    width = t_resid.shape[1]
    piece = (1, 8, tok, width)
    blocks = [(a, piece, (0, 0, 0, 0)) for a in (mine, came)]
    up, down_ = on_blocks(far_body, [shape(4, tok, width)] * 2, blocks)
    up, down_ = tied(moved_by(up, "y", 1), moved_by(down_, "y", -1))
    blocks = [(a, piece, (d, 0, 0, 0)) for d in (3, 1, 2) for a in (mine, came)]
    near_up, near_down, chip = on_blocks(chip_body, [shape(8, tok, width)] * 3, blocks)
    student, near_up, near_down, chip = tied(student, near_up, near_down, chip)
    hidden = call(hidden_body, [shape(4, tok, cols)], [student, resid])[0]
    ups = call(near_body, [shape(8, tok, width)] * 2, [near_up, near_down, up, down_])
    hidden, *ups = tied(hidden, *ups)
    hidden = exchanged(hidden, "zl")
    pair = tied(pair, hidden)[0]
    ups = tied(moved_by(ups[0], "y", 1), moved_by(ups[1], "y", -1))

    next_, last_ = tied(moved_by(pair, "x", -1), moved_by(pair, "x", 1))
    far_rows = tied(moved_by(next_[0], "x", -1), moved_by(last_[1], "x", 1))

    over = call(terms_body, [shape(8, tok, width)], [chip, *ups])[0]
    over, hidden = tied(over, hidden)
    terms = exchanged(over, Z)
    hidden = jnp.concatenate(
        [hidden, *tied(*(moved_by(hidden, "y", -step) for step in (1, 2, 3)))], axis=0
    )
    rows = [pair, next_, last_, *far_rows]
    rows = rows + [swapped(r, "c") for r in rows]

    mapped, rows = call(
        mapped_body,
        [shape(*t_resid.shape, dtype=F32), shape(16, *proj.shape)],
        [at_cols, hidden, *rows],
        [SMEM] + [VMEM] * 11,
    )
    mapped, terms = tied(mapped, terms)
    err, back = call(
        err_body,
        [shape(*t_resid.shape), shape(4, 4, tok, cols)],
        [at_cols, mapped, t_resid, terms, rows],
        [SMEM] + [VMEM] * 4,
    )
    back_moved = tied(*(moved_by(back[step], "y", step) for step in (1, 2, 3)))

    scale = 1.0 / math.sqrt(tok * 16)
    theirs_g = call(
        functools.partial(grad_body, scale, 8),
        [shape(8, *proj.shape)],
        [at_cols, hidden, err],
        [SMEM, VMEM, VMEM],
    )[0]
    came_g = swapped(theirs_g, "c")
    near_g, left_g, right_g, far_up, far_down = call(
        functools.partial(grad_body, scale, 0),
        [shape(2, *proj.shape)] * 3 + [shape(*proj.shape)] * 2,
        [at_cols, hidden, err, came_g],
        [SMEM, VMEM, VMEM, VMEM],
    )
    far_up, far_down = moved_by(far_up, "x", 1), moved_by(far_down, "x", -1)
    moved_g = call(grad_near_body, [shape(2, *proj.shape)] * 2, [left_g, right_g, far_up, far_down])
    *back_moved, up_g, down_g = tied(*back_moved, *moved_g)
    moved_g = [up_g, down_g]
    moved_g = [moved_by(moved_g[0], "x", 1), moved_by(moved_g[1], "x", -1)]

    back = call(terms_body, [shape(4, tok, cols)], [back[0], *back_moved])[0]
    back = exchanged(back, "zl")
    back = call(sum_body, [shape(4, tok, cols)], [back])[0]
    back = exchanged(back, "zl")
    back, *moved_g = tied(back, *moved_g)
    back_all = [back, *tied(*(moved_by(back, "y", -step) for step in (1, 2, 3)))]

    own_g, sent_g = call(
        grad_sum_body, [shape(*proj.shape, dtype=F32), shape(*proj.shape)], [near_g, *moved_g]
    )
    came_g = swapped(sent_g, "zh")
    attn_grad = call(attn_body, [shape(tok, cols)], [here, out_proj, *back_all], [SMEM] + [VMEM] * 5)[0]
    attn_grad, came_g = tied(attn_grad, came_g)
    proj_grad = own_g + came_g.astype(F32)
    return (attn_grad, proj_grad)


def solution(mesh):
    fine = Mesh(mesh.devices.reshape(2, 2, 4, 4, 4), ("zh", "c", "x", "y", "zl"))
    group, tensor = ("zh", "c", "x"), ("y", "zl")
    hidden_units = ("zh", "c", "y", "zl")
    return jax.shard_map(
        on_device,
        mesh=fine,
        in_specs=(
            P(None, "x", hidden_units),
            P(hidden_units, None),
            P(group, tensor),
            P(group, tensor),
            P(tensor, None),
            P(group, None),
            P(group, tensor),
        ),
        out_specs=(P(group, tensor), P(group, tensor)),
        check_vma=False,
    )
```
